32 devices in a mesh: layer: 2 (over x), row: 4 (over z), col: 4 (over y, core).
Axes of the slice: x: 2, y: 2, z: 4, core: 2. Of those that a mesh axis runs over, the one named last changes fastest.
Arguments:
- slab_tiles: bfloat16 [128, 16, 2, 4, 128], P(None, 'row', 'layer'), may hold values from -0.0546875 to 0.0546875
- x_tiles: bfloat16 [32, 4, 2, 128, 128], P(('layer', 'row', 'col')), may hold values from -6 to 6
- x_cols: int32 [32, 4, 2], P(('layer', 'row', 'col')), may hold values from 0 to 31, as said below
- x2_tiles: bfloat16 [32, 4, 2, 128, 128], P(('layer', 'row', 'col')), may hold values from -6 to 6
- x2_cols: int32 [32, 4, 2], P(('layer', 'row', 'col')), may hold values from 0 to 31, as said below
- requests: int32 [2, 4, 4], P('layer'), may hold values from 0 to 31, as said below
- out_cols: int32 [4, 4, 4], P('row', 'col'), may hold values from 0 to 31, as said below
Outputs:
- purified: bfloat16 [128, 16, 4, 4, 128], P('layer', 'row', 'col')
The draws below stay inside these ranges and needn't reach their ends.
Inputs may be any that keep to these rules, and one draw needn't show every extreme that they name: Block row k is held by the device at index k of layer, row and col taken together. requests[l, r, q] is a block row held by layer l at row index (r + q * 1) % 4; every block row held by layer l is named exactly once in requests[l]. out_cols[r, c] holds 4 distinct block columns j, each with j % 4 == c. x_cols[k, c] holds 2 distinct block columns taken from out_cols[r, c], where r is the group whose requests name k. x2_cols[k, c] holds 2 distinct block columns taken from out_cols[r, c], where r is the group whose requests name k.
All inputs are finite; a program needn't handle non-finite values.
Results may differ from the reference program's by a relative error of at most 0.001.
Values may be sent and summed in bfloat16 or wider, within the bound.
No kernel may reach another device: no remote copies, remote signals or barrier semaphores. Data moves between devices by JAX's collectives and lax.ppermute only.
A program may use at most 64 MiB of HBM per device.

```python
import jax
import jax.numpy as jnp
from jax import lax

BS = 128
SR = 4
NZC = 2
NOUT = 4
NB = 32
REQ = 4
SLAB = 16
N_LAYER = 2
N_ROW = 4
N_COL = 4


def build_requests(key):
    order_keys = jax.random.split(jax.random.fold_in(key, 202), N_LAYER * N_ROW)

    def col_order(sub_key):
        return jax.random.permutation(sub_key, N_COL)
    orders = jax.vmap(col_order)(order_keys).reshape(N_LAYER, N_ROW, N_COL)
    layer_ids = jnp.arange(N_LAYER, dtype=jnp.int32)[:, None, None]
    group_ids = jnp.arange(N_ROW, dtype=jnp.int32)[None, :, None]
    slot_ids = jnp.arange(N_COL, dtype=jnp.int32)[None, None, :]
    owner_rows = (group_ids + slot_ids * (N_ROW // N_COL)) % N_ROW
    owner_cols = orders[layer_ids, owner_rows, slot_ids]
    return ((layer_ids * N_ROW + owner_rows) * N_COL + owner_cols).astype(jnp.int32)


def build_out_cols(key):
    pair_keys = jax.random.split(jax.random.fold_in(key, 303), N_ROW * N_COL)

    def pick_cols(sub_key):
        return jax.random.permutation(sub_key, N_LAYER * N_ROW)[:NOUT]
    chosen = jax.vmap(pick_cols)(pair_keys).reshape(N_ROW, N_COL, NOUT)
    return (chosen * N_COL + jnp.arange(N_COL, dtype=jnp.int32)[None, :, None]).astype(jnp.int32)


def build_cols(key, salt_value):
    requests = build_requests(key)
    targets = build_out_cols(key)
    group_ids = jnp.broadcast_to(jnp.arange(N_ROW, dtype=jnp.int32)[None, :, None], requests.shape)
    group_of = jnp.zeros((NB,), jnp.int32).at[requests.reshape(-1)].set(group_ids.reshape(-1))
    slot_keys = jax.random.split(jax.random.fold_in(key, salt_value), NB * N_COL)

    def pick_slots(sub_key):
        return jax.random.permutation(sub_key, NOUT)[:NZC]
    slot_picks = jax.vmap(pick_slots)(slot_keys).reshape(NB, N_COL, NZC)
    column_ids = jnp.arange(N_COL, dtype=jnp.int32)[None, :, None]
    return targets[group_of[:, None, None], column_ids, slot_picks].astype(jnp.int32)


def draw_requests(key, part):
    return build_requests(key)


def draw_out_cols(key, part):
    return build_out_cols(key)


def draw_x_cols(key, part):
    return build_cols(key, 404)


def draw_x2_cols(key, part):
    return build_cols(key, 505)


def shard_levels(own_key, dims, shards, least, top_value):
    level = 1.0
    for axis_at, shards_of in shards:
        draws = jax.random.uniform(jax.random.fold_in(jax.random.fold_in(own_key, 6), axis_at), (shards_of,), jnp.float32, least / len(shards), top_value / len(shards))
        level = level * jnp.repeat(jnp.exp(draws), dims[axis_at] // shards_of).reshape((-1,) + (1,) * (len(dims) - 1 - axis_at))
    return level


def centred(rng, shape, spread, limit, cuts=(), held_as=jnp.bfloat16):
    gain = shard_levels(rng, shape, cuts, -0.22, 0.18) if cuts else 1.0
    values = jax.random.normal(rng, shape, jnp.float32) * spread * gain
    return jnp.minimum(jnp.maximum(values, -limit), limit).astype(held_as)


def setup_inputs(seed: int = 0) -> dict:
    arg_keys = jax.random.split(jax.random.key(seed), 8)
    return {
        "slab_tiles": centred(arg_keys[0], (BS, SLAB, N_LAYER, REQ, BS), (25 * N_LAYER * N_COL * BS * NZC // NOUT) ** -0.5, 0.0546875, ((1, 4), (2, 2))),
        "x_tiles": centred(arg_keys[1], (NB, N_COL, NZC, BS, BS), 1.0, 6.0, ((0, 32),)),
        "x_cols": draw_x_cols(jax.random.fold_in(arg_keys[7], 71), 0),
        "x2_tiles": centred(arg_keys[3], (NB, N_COL, NZC, BS, BS), 1.0, 6.0, ((0, 32),)),
        "x2_cols": draw_x2_cols(jax.random.fold_in(arg_keys[7], 71), 0),
        "requests": draw_requests(jax.random.fold_in(arg_keys[7], 71), 0),
        "out_cols": draw_out_cols(jax.random.fold_in(arg_keys[7], 71), 0),
    }


def choose_tiles(tile_set, col_ids, picked, targets):
    gathered = tile_set[picked].astype(jnp.float32)
    listed = col_ids[picked]
    matches = (listed[:, :, :, None] == targets[None, :, None, :]).astype(jnp.float32)
    chosen = jnp.einsum('kcus,kcubd->kbcsd', matches, gathered)
    return chosen.astype(jnp.bfloat16).reshape(picked.shape[0] * BS, N_COL * NOUT * BS)


def reference(slab_tiles, x_tiles, x_cols, x2_tiles, x2_cols, requests, out_cols):
    def one_group(grid_row):
        picked = lax.dynamic_index_in_dim(requests, grid_row, 1, keepdims=False).reshape(-1).astype(jnp.int32)
        targets = lax.dynamic_index_in_dim(out_cols, grid_row, 0, keepdims=False)
        a_block = lax.dynamic_slice_in_dim(slab_tiles, (grid_row * SR).astype(jnp.int32), SR, 1)
        a_block = a_block.reshape(BS * SR, N_LAYER * REQ * BS)
        first_term = jnp.dot(a_block, choose_tiles(x_tiles, x_cols, picked, targets), preferred_element_type=jnp.float32)
        second_term = jnp.dot(a_block, choose_tiles(x2_tiles, x2_cols, picked, targets), preferred_element_type=jnp.float32)
        combined = (4.0 * first_term - 3.0 * second_term).astype(jnp.bfloat16)
        return combined.reshape(BS, SR, N_COL, NOUT, BS)

    blocks = lax.map(one_group, jnp.arange(N_ROW, dtype=jnp.int32))
    return jnp.transpose(blocks, (1, 0, 2, 3, 4, 5)).reshape(BS, SLAB, N_COL, NOUT, BS)
```

```python
import functools

import jax
import jax.numpy as jnp
from jax import lax
from jax.experimental import pallas as pl
from jax.experimental.pallas import tpu as pltpu
from jax.sharding import PartitionSpec as P

DIGIT = 8
VMEM = pl.BlockSpec(memory_space=pltpu.VMEM)
SMEM = pl.BlockSpec(memory_space=pltpu.SMEM)


def mate(index, step, size):
    return index ^ step if size & (size - 1) == 0 else (index - step) % size


def target(index, step, size):
    return index ^ step if size & (size - 1) == 0 else (index + step) % size


def round_of(index, source, size):
    return index ^ source if size & (size - 1) == 0 else lax.rem(index - source + size, size)


def exchange(block, axis, step, size, stride=1):
    route = []
    for place in range(size * stride):
        high, low = divmod(place, stride)
        route.append((place, target(high, step, size) * stride + low))
    return lax.ppermute(block, axis, route)


def id_rows(stored):
    return -(-4 * stored // 16) * 16


def pack_kernel(x_ref, x2_ref, cols_ref, cols2_ref, *outs):
    groups, stored, side = x_ref.shape[1:4]
    own = lax.axis_index("col")
    count = id_rows(stored)
    row = lax.broadcasted_iota(jnp.int32, (count, side), 0)
    for step, out in enumerate(outs):
        reader = target(own, step, groups)
        digits = jnp.zeros((count, side), jnp.int32)
        for part, (ref, cols) in enumerate(((x_ref, cols_ref), (x2_ref, cols2_ref))):
            for at in range(stored):
                place = part * stored + at
                out[pl.ds(place * side, side), :] = ref[0, reader, at]
                value = cols[0, at, reader]
                digits = jnp.where(row == 2 * place, value >> DIGIT, digits)
                digits = jnp.where(row == 2 * place + 1, value & ((1 << DIGIT) - 1), digits)
        out[pl.ds(2 * stored * side, count), :] = digits.astype(jnp.float32).astype(out.dtype)


def pack(x_tiles, x2_tiles, x_cols, x2_cols):
    _, groups, stored, side, _ = x_tiles.shape
    shape = jax.ShapeDtypeStruct((2 * stored * side + id_rows(stored), side), x_tiles.dtype)
    return pl.pallas_call(
        pack_kernel,
        out_shape=[shape] * groups,
        in_specs=[VMEM, VMEM, SMEM, SMEM],
        out_specs=[VMEM] * groups,
        name="pack",
    )(x_tiles, x2_tiles, jnp.swapaxes(x_cols, 1, 2), jnp.swapaxes(x2_cols, 1, 2))


def pick_kernel(stride, wanted_ref, *rest):
    groups = len(rest) // 2
    held, outs = rest[:groups], rest[groups:]
    own_row, own_col = lax.axis_index("row"), lax.axis_index("col")
    high, low = own_row // stride, own_row % stride
    for step, out in enumerate(outs):
        reader = target(high, step, groups)
        slot = lax.rem(high - reader + groups, groups)
        owner = lax.rem(wanted_ref[0, reader * stride + low, slot], groups)
        came = round_of(own_col, owner, groups)
        for at in range(groups):

            @pl.when(came == at)
            def _(at=at, out=out):
                out[...] = held[at][...]


def pick(requests, held, stride):
    groups = len(held)
    return pl.pallas_call(
        functools.partial(pick_kernel, stride),
        out_shape=[jax.ShapeDtypeStruct(held[0].shape, held[0].dtype)] * groups,
        in_specs=[SMEM] + [VMEM] * groups,
        out_specs=[VMEM] * groups,
        name="pick",
    )(requests, *held)


def split_kernel(slots, slab_ref, *rest):
    outs, wide = rest[:-1], rest[-1]
    layers = len(outs)
    rows = slab_ref.shape[0] // layers
    own = lax.axis_index("layer")
    for step, out in enumerate(outs):
        part = target(own, step, layers)
        first = pl.multiple_of(part * rows, rows)
        wide[...] = slab_ref[pl.ds(first, rows)].astype(jnp.float32)
        for slot in range(slots):
            out[slot] = wide[pl.ds(slot, rows // slots, stride=slots)].astype(out.dtype)


def split(slab_tiles, layers):
    high, per, _, slots, side = slab_tiles.shape
    rows = high * per // layers
    flat = slab_tiles.reshape(high * per * slots, side)
    return pl.pallas_call(
        functools.partial(split_kernel, slots),
        out_shape=[jax.ShapeDtypeStruct((slots, rows, side), slab_tiles.dtype)] * layers,
        in_specs=[VMEM],
        out_specs=[VMEM] * layers,
        scratch_shapes=[pltpu.VMEM((rows * slots, side), jnp.float32)],
        name="split",
    )(flat)


def product_kernel(stride, layers, stored, targets_ref, *rest):
    out_ref, tall = rest[-2:]
    lefts, rest = rest[:layers], rest[layers:-2]
    groups = len(rest) // layers
    slots, rows, side = lefts[0].shape
    wanted = targets_ref.shape[2]
    high = lax.axis_index("row") // stride
    left_parts, first_parts, second_parts = [], [], []
    for layer in range(layers):
        for step in range(groups):
            slot = lax.rem(mate(high, step, groups) - high + groups, groups)
            left_parts.append(lefts[layer][slot])
            block = rest[layer * groups + step]
            digits = block[pl.ds(2 * stored * side, id_rows(stored)), :].astype(jnp.float32)
            for part, into in enumerate((first_parts, second_parts)):
                across = [jnp.zeros((side, side), jnp.bfloat16)] * wanted
                for at in range(stored):
                    place = part * stored + at
                    tile = block[pl.ds(place * side, side), :]
                    listed = (
                        digits[2 * place : 2 * place + 1] * (1 << DIGIT)
                        + digits[2 * place + 1 : 2 * place + 2]
                    )
                    for s in range(wanted):
                        goal = targets_ref[0, 0, s].astype(jnp.float32)
                        hit = jnp.broadcast_to(jnp.where(listed == goal, 1.0, 0.0), (side, side))
                        across[s] = across[s] + tile * hit.astype(jnp.bfloat16)
                into.append(jnp.concatenate(across, axis=1))
    left = jnp.concatenate(left_parts, axis=1)
    first = jnp.dot(left, jnp.concatenate(first_parts, axis=0), preferred_element_type=jnp.float32)
    second = jnp.dot(left, jnp.concatenate(second_parts, axis=0), preferred_element_type=jnp.float32)
    summed = 4.0 * first - 3.0 * second
    for s in range(wanted):
        tall[pl.ds(s, rows, stride=wanted)] = summed[:, s * side : (s + 1) * side]
    out_ref[...] = tall[...].astype(out_ref.dtype)


def product(lefts, blocks, targets, stored, stride):
    layers = len(lefts)
    _, rows, side = lefts[0].shape
    wanted = targets.shape[2]
    flat = [block for of_layer in blocks for block in of_layer]
    return pl.pallas_call(
        functools.partial(product_kernel, stride, layers, stored),
        out_shape=jax.ShapeDtypeStruct((rows * wanted, side), lefts[0].dtype),
        in_specs=[SMEM] + [VMEM] * (layers + len(flat)),
        out_specs=VMEM,
        scratch_shapes=[pltpu.VMEM((rows * wanted, side), jnp.float32)],
        compiler_params=pltpu.CompilerParams(vmem_limit_bytes=32 * 1024 * 1024),
        name="product",
    )(targets, *lefts, *flat)


def body(slab_tiles, x_tiles, x_cols, x2_tiles, x2_cols, requests, out_cols):
    layers, rows, groups = (lax.axis_size(axis) for axis in ("layer", "row", "col"))
    stride = rows // groups
    stored = x_tiles.shape[2]
    packed = pack(x_tiles, x2_tiles, x_cols, x2_cols)
    held = [packed[0]] + [exchange(packed[k], "col", k, groups) for k in range(1, groups)]
    lefts = split(slab_tiles, layers)
    lefts = [lefts[0]] + [exchange(lefts[k], "layer", k, layers) for k in range(1, layers)]
    picked = pick(requests, held, stride)
    got = [picked[0]] + [exchange(picked[k], "row", k, groups, stride) for k in range(1, groups)]
    blocks = [got] + [[exchange(block, "layer", k, layers) for block in got] for k in range(1, layers)]
    out = product(lefts, blocks, out_cols, stored, stride)
    high, per = slab_tiles.shape[0] // layers, slab_tiles.shape[1]
    return out.reshape(high, per, 1, out_cols.shape[2], x_tiles.shape[4])


def solution(mesh):
    placed = (
        P(None, "row", "layer", None, None),
        P(("layer", "row", "col"), None, None, None, None),
        P(("layer", "row", "col"), None, None),
        P(("layer", "row", "col"), None, None, None, None),
        P(("layer", "row", "col"), None, None),
        P("layer", None, None),
        P("row", "col", None),
    )
    return jax.shard_map(
        body,
        mesh=mesh,
        in_specs=placed,
        out_specs=P("layer", "row", "col", None, None),
        check_vma=False,
    )
```

```python
import functools

import jax
import jax.numpy as jnp
from jax import lax
from jax.experimental import pallas as pl
from jax.experimental.pallas import tpu as pltpu
from jax.sharding import PartitionSpec as P

DIGIT = 8
VMEM = pl.BlockSpec(memory_space=pltpu.VMEM)
SMEM = pl.BlockSpec(memory_space=pltpu.SMEM)
HBM = pl.BlockSpec(memory_space=pltpu.HBM)
SMALL = pltpu.CompilerParams(vmem_limit_bytes=8 * 1024 * 1024)


def mate(index, step, size):
    return index ^ step if size & (size - 1) == 0 else (index - step) % size


def target(index, step, size):
    return index ^ step if size & (size - 1) == 0 else (index + step) % size


def round_of(index, source, size):
    return index ^ source if size & (size - 1) == 0 else lax.rem(index - source + size, size)


def exchange(block, axis, step, size, stride=1):
    route = []
    for place in range(size * stride):
        high, low = divmod(place, stride)
        route.append((place, target(high, step, size) * stride + low))
    return lax.ppermute(block, axis, route)


def id_rows(stored):
    return -(-4 * stored // 16) * 16


def pack_kernel(stride, x_far, x2_far, *rest):
    groups, stored, side = x_far.shape[1:4]
    fars, outs, (choice, goals) = rest[:4], rest[4 : 4 + groups], rest[4 + groups : 6 + groups]
    nears, (sems, id_sems) = rest[6 + groups : 10 + groups], rest[10 + groups :]
    cols_ref, cols2_ref, wanted_ref, goals_ref = nears
    own = lax.axis_index("col")
    ids = [
        pltpu.make_async_copy(far, near, id_sems.at[at]) for at, (far, near) in enumerate(zip(fars, nears))
    ]
    loads = [
        pltpu.make_async_copy(
            far.at[0, target(own, step, groups), at],
            out.at[pl.ds((part * stored + at) * side, side)],
            sems.at[step, part * stored + at],
        )
        for step, out in enumerate(outs)
        for part, far in enumerate((x_far, x2_far))
        for at in range(stored)
    ]
    for load in ids + loads:
        load.start()
    for load in ids:
        load.wait()
    count = id_rows(stored)
    row = lax.broadcasted_iota(jnp.int32, (count, side), 0)
    for step, out in enumerate(outs):
        reader = target(own, step, groups)
        digits = jnp.zeros((count, side), jnp.int32)
        for part, cols in enumerate((cols_ref, cols2_ref)):
            for at in range(stored):
                value, place = cols[0, at, reader], 2 * (part * stored + at)
                digits = jnp.where(row == place, value >> DIGIT, digits)
                digits = jnp.where(row == place + 1, value & ((1 << DIGIT) - 1), digits)
        out[pl.ds(2 * stored * side, count), :] = digits.astype(jnp.float32).astype(out.dtype)
    own_row = lax.axis_index("row")
    high, low = own_row // stride, own_row % stride
    row = lax.broadcasted_iota(jnp.int32, choice.shape, 0)
    came = jnp.zeros(choice.shape, jnp.int32)
    for step in range(groups):
        reader = target(high, step, groups)
        slot = lax.rem(high - reader + groups, groups)
        owner = lax.rem(wanted_ref[0, reader * stride + low, slot], groups)
        came = jnp.where(row // groups == step, round_of(own, owner, groups), came)
    choice[...] = jnp.where(row % groups == came, 1.0, 0.0)
    row = lax.broadcasted_iota(jnp.int32, goals.shape, 0)
    goal = jnp.zeros(goals.shape, jnp.int32)
    for s in range(goals_ref.shape[2]):
        goal = jnp.where(row == s, goals_ref[0, 0, s], goal)
    goals[...] = goal.astype(jnp.float32)
    for load in loads:
        load.wait()


def pinned(array):
    return pltpu.with_memory_space_constraint(array, pltpu.HBM)


def pack(x_tiles, x2_tiles, x_cols, x2_cols, requests, out_cols, stride):
    _, groups, stored, side, _ = x_tiles.shape
    kind = x_tiles.dtype
    small = (jnp.swapaxes(x_cols, 1, 2), jnp.swapaxes(x2_cols, 1, 2), requests, out_cols)
    out = pl.pallas_call(
        functools.partial(pack_kernel, stride),
        out_shape=[jax.ShapeDtypeStruct((2 * stored * side + id_rows(stored), side), kind)] * groups
        + [
            jax.ShapeDtypeStruct((groups * groups, side), jnp.float32),
            jax.ShapeDtypeStruct((-(-out_cols.shape[2] // 8) * 8, side), jnp.float32),
        ],
        in_specs=[HBM] * 6,
        out_specs=[VMEM] * (groups + 2),
        scratch_shapes=[pltpu.SMEM(array.shape, array.dtype) for array in small]
        + [pltpu.SemaphoreType.DMA((groups, 2 * stored)), pltpu.SemaphoreType.DMA((len(small),))],
        compiler_params=SMALL,
        name="pack",
    )(pinned(x_tiles), pinned(x2_tiles), *map(pinned, small))
    return list(out[:groups]), *out[groups:]


def split_kernel(slots, slab_far, _, own_ref, *rest):
    outs, (wide, slab_ref, sems) = rest[:-3], rest[-3:]
    layers, pieces = len(outs) + 1, sems.shape[0]
    rows = slab_far.shape[0] // layers
    share = rows // pieces
    own, parity = lax.axis_index("layer"), lax.axis_index("col") % 2
    firsts = [target(own, step, layers) * rows for step in range(layers)]
    loads = [
        [
            pltpu.make_async_copy(
                slab_far.at[pl.ds(pl.multiple_of(first + at * share, share), share)],
                slab_ref.at[step, pl.ds(at * share, share)],
                sems.at[at, step],
            )
            for at in range(pieces)
        ]
        for step, first in enumerate(firsts)
    ]
    for load in sum(loads, []):
        load.start()
    for step in reversed(range(layers)):
        for load in loads[step]:
            load.wait()
        wide[...] = slab_ref[step].astype(jnp.float32)
        if step:
            half = slots // 2
            for slot in range(half):
                picked = wide[pl.ds(parity * half + slot, rows // slots, stride=slots)]
                outs[step - 1][slot] = picked.astype(own_ref.dtype)
        else:
            for slot in range(slots):
                own_ref[slot] = wide[pl.ds(slot, rows // slots, stride=slots)].astype(own_ref.dtype)


def split(slab_tiles, after, layers):
    high, per, _, slots, side = slab_tiles.shape
    rows = high * per // layers
    kind = slab_tiles.dtype
    out = pl.pallas_call(
        functools.partial(split_kernel, slots),
        out_shape=[jax.ShapeDtypeStruct((slots, rows, side), kind)]
        + [jax.ShapeDtypeStruct((slots // 2, rows, side), kind)] * (layers - 1),
        in_specs=[HBM, pl.BlockSpec(memory_space=pl.ANY)],
        out_specs=[VMEM] * layers,
        scratch_shapes=[
            pltpu.VMEM((rows * slots, side), jnp.float32),
            pltpu.VMEM((layers, rows * slots, side), kind),
            pltpu.SemaphoreType.DMA((4, layers)),
        ],
        compiler_params=SMALL,
        name="split",
    )(pinned(slab_tiles.reshape(high * per * slots, side)), after)
    return out[0], list(out[1:])


def pick_kernel(cuts, choice, *rest):
    groups = len(cuts)
    held, outs = rest[:groups], list(rest[groups:])
    side = choice.shape[1]
    for step, sizes in enumerate(cuts):
        first = 0
        for size in sizes:
            out = outs.pop(0)
            total = jnp.zeros((size, side), out.dtype)
            for at in range(groups):
                place = step * groups + at
                hit = jnp.broadcast_to(choice[place : place + 1, :], (size, side)).astype(out.dtype)
                total += held[at][pl.ds(first, size), :] * hit
            out[...] = total
            first += size


def pick(choice, held, cuts):
    side, kind = held[0].shape[1], held[0].dtype
    sizes = [size for cut in cuts for size in cut]
    out = pl.pallas_call(
        functools.partial(pick_kernel, cuts),
        out_shape=[jax.ShapeDtypeStruct((size, side), kind) for size in sizes],
        in_specs=[VMEM] * (1 + len(held)),
        out_specs=[VMEM] * len(sizes),
        compiler_params=SMALL,
        name="pick",
    )(choice, *held)
    out = iter(out)
    return [[next(out) for _ in cut] for cut in cuts]


def product_kernel(stride, layers, stored, rounds, cuts, wanted, last, goals, *rest):
    lefts, rest = rest[: 2 * layers - 1], list(rest[2 * layers - 1 :])
    groups = len(cuts)
    slots, rows, side = lefts[0].shape
    half = slots // 2
    high, parity = lax.axis_index("row") // stride, lax.axis_index("col") % 2
    left_parts, sums = [], ([], [])
    for layer in range(layers):
        for step in rounds:
            slot = lax.rem(mate(high, step, groups) - high + groups, groups)
            if layer:
                same, other = lefts[2 * layer - 1], lefts[2 * layer]
                at = lax.rem(slot, half)
                left_parts.append(jnp.where(slot // half == parity, same[at], other[at]))
            else:
                left_parts.append(lefts[0][slot])
            pieces, rest = rest[: len(cuts[step])], rest[len(cuts[step]) :]

            def fetch(first, size, pieces=pieces):
                for piece in pieces:
                    if first < piece.shape[0]:
                        return piece[pl.ds(first, size), :]
                    first -= piece.shape[0]

            digits = fetch(2 * stored * side, id_rows(stored)).astype(jnp.float32)
            for part, into in enumerate(sums):
                across = [jnp.zeros((side, side), jnp.bfloat16)] * wanted
                for at in range(stored):
                    place = part * stored + at
                    tile = fetch(place * side, side)
                    listed = (
                        digits[2 * place : 2 * place + 1] * (1 << DIGIT)
                        + digits[2 * place + 1 : 2 * place + 2]
                    )
                    for s in range(wanted):
                        hit = jnp.where(listed == goals[s : s + 1, :], 1.0, 0.0)
                        hit = jnp.broadcast_to(hit, (side, side))
                        across[s] = across[s] + tile * hit.astype(jnp.bfloat16)
                into.append(jnp.concatenate(across, axis=1))
    left = jnp.concatenate(left_parts, axis=1)
    first, second = (
        jnp.dot(left, jnp.concatenate(chosen, axis=0), preferred_element_type=jnp.float32) for chosen in sums
    )
    summed = 4.0 * first - 3.0 * second
    if last:
        tall = rest.pop()
    out_ref = rest.pop()
    if rest:
        summed += rest.pop()[...]
    if last:
        for s in range(wanted):
            tall[pl.ds(s, rows, stride=wanted)] = summed[:, s * side : (s + 1) * side]
        summed = tall[...]
    out_ref[...] = summed.astype(out_ref.dtype)


def product(lefts, blocks, total, goals, wanted, stored, stride, rounds, cuts, last):
    layers = len(blocks)
    _, rows, side = lefts[0].shape
    flat = [piece for of_layer in blocks for step in rounds for piece in of_layer[step]]
    flat += [] if total is None else [total]
    shape = (rows * wanted, side) if last else (rows, wanted * side)
    return pl.pallas_call(
        functools.partial(product_kernel, stride, layers, stored, rounds, cuts, wanted, last),
        out_shape=jax.ShapeDtypeStruct(shape, lefts[0].dtype if last else jnp.float32),
        in_specs=[VMEM] * (1 + len(lefts) + len(flat)),
        out_specs=VMEM,
        scratch_shapes=[pltpu.VMEM(shape, jnp.float32)] if last else [],
        compiler_params=pltpu.CompilerParams(vmem_limit_bytes=16 * 1024 * 1024),
        name="product",
    )(goals, *lefts, *flat)


def body(slab_tiles, x_tiles, x_cols, x2_tiles, x2_cols, requests, out_cols):
    layers, rows, groups = (lax.axis_size(axis) for axis in ("layer", "row", "col"))
    stride = rows // groups
    _, _, stored, side, _ = x_tiles.shape
    half, whole = stored * side, 2 * stored * side + id_rows(stored)
    order = [0, *reversed(range(3, groups)), 1, 2]
    cuts = [(half, whole - half) if k == order[-1] else (whole,) for k in range(groups)]
    packed, choice, goals = pack(x_tiles, x2_tiles, x_cols, x2_cols, requests, out_cols, stride)
    held = [packed[0]] + [exchange(packed[k], "col", k, groups) for k in range(1, groups)]
    own, sent = split(slab_tiles, held[1], layers)
    lefts = [exchange(sent[k - 1], "layer", k, layers) for k in range(1, layers)]
    held, lefts = lax.optimization_barrier((held, lefts))
    lefts = [own] + [left for same in lefts for left in (same, exchange(same, "col", 1, groups))]
    picked = pick(choice, held, cuts)
    got = [picked[0]] + [None] * (groups - 1)
    for k in order[1:]:
        got[k] = [exchange(piece, "row", k, groups, stride) for piece in picked[k]]
    blocks = [got] + [[None] * groups for _ in range(1, layers)]

    def forward(k, after):
        mine, _ = lax.optimization_barrier((got[k], after))
        for step in range(1, layers):
            blocks[step][k] = [exchange(piece, "layer", step, layers) for piece in mine]

    def add(total, rounds, last):
        return product(lefts, blocks, total, goals, out_cols.shape[2], stored, stride, rounds, cuts, last)

    forward(0, ())
    for k in order[1:]:
        forward(k, blocks[-1][0])
    total = add(None, order[:2], False)
    for k in order[2:-1]:
        total = add(total, [k], False)
    total = add(total, order[-1:], True)
    high, per = slab_tiles.shape[0] // layers, slab_tiles.shape[1]
    return total.reshape(high, per, 1, out_cols.shape[2], side)


def solution(mesh):
    placed = (
        P(None, "row", "layer", None, None),
        P(("layer", "row", "col"), None, None, None, None),
        P(("layer", "row", "col"), None, None),
        P(("layer", "row", "col"), None, None, None, None),
        P(("layer", "row", "col"), None, None),
        P("layer", None, None),
        P("row", "col", None),
    )
    return jax.shard_map(
        body,
        mesh=mesh,
        in_specs=placed,
        out_specs=P("layer", "row", "col", None, None),
        check_vma=False,
    )
```

```python
import functools

import jax
import jax.numpy as jnp
from jax import lax
from jax.experimental import pallas as pl
from jax.experimental.pallas import tpu as pltpu
from jax.sharding import PartitionSpec as P

WHOLE = 2
DIGIT = 8
VMEM = pl.BlockSpec(memory_space=pltpu.VMEM)
SMEM = pl.BlockSpec(memory_space=pltpu.SMEM)
HBM = pl.BlockSpec(memory_space=pltpu.HBM)
SMALL = pltpu.CompilerParams(vmem_limit_bytes=8 * 1024 * 1024)


def mate(index, step, size):
    return index ^ step if size & (size - 1) == 0 else (index - step) % size


def target(index, step, size):
    return index ^ step if size & (size - 1) == 0 else (index + step) % size


def round_of(index, source, size):
    return index ^ source if size & (size - 1) == 0 else lax.rem(index - source + size, size)


def exchange(block, axis, step, size, stride=1):
    route = []
    for place in range(size * stride):
        high, low = divmod(place, stride)
        route.append((place, target(high, step, size) * stride + low))
    return lax.ppermute(block, axis, route)


def id_rows(stored):
    return -(-4 * stored // 16) * 16


def rows_of(span, stored, side):
    return (span[1] - span[0]) * side + (id_rows(stored) if span[1] == 2 * stored else 0)


def find(pieces, spans, block, side):
    for piece, (low, high) in zip(pieces, spans):
        if low <= block < high:
            return piece, (block - low) * side


def pack_kernel(stride, spans, x_far, x2_far, *rest):
    groups, stored, side = x_far.shape[1:4]
    fars, rest = rest[:4], list(rest[4:])
    outs = [[rest.pop(0) for _ in cut] for cut in spans]
    (choice, goals), nears, (sems, id_sems) = rest[:2], rest[2:-2], rest[-2:]
    cols_ref, cols2_ref, wanted_ref, goals_ref = nears
    count = id_rows(stored)
    own = lax.axis_index("col")
    ids = [
        pltpu.make_async_copy(far, near, id_sems.at[at]) for at, (far, near) in enumerate(zip(fars, nears))
    ]
    loads = []
    for step, out in enumerate(outs):
        reader = target(own, step, groups)
        for block in range(2 * stored):
            piece, first = find(out, spans[step], block, side)
            far = (x_far, x2_far)[block // stored].at[0, reader, block % stored]
            loads.append(pltpu.make_async_copy(far, piece.at[pl.ds(first, side)], sems.at[step, block]))
    for load in ids + loads:
        load.start()
    for load in ids:
        load.wait()
    row = lax.broadcasted_iota(jnp.int32, (count, side), 0)
    for step, out in enumerate(outs):
        reader = target(own, step, groups)
        digits = jnp.zeros((count, side), jnp.int32)
        for block in range(2 * stored):
            value = (cols_ref, cols2_ref)[block // stored][0, block % stored, reader]
            digits = jnp.where(row == 2 * block, value >> DIGIT, digits)
            digits = jnp.where(row == 2 * block + 1, value & ((1 << DIGIT) - 1), digits)
        first = out[-1].shape[0] - count
        out[-1][pl.ds(first, count), :] = digits.astype(jnp.float32).astype(out[-1].dtype)
    own_row = lax.axis_index("row")
    high, low = own_row // stride, own_row % stride
    row = lax.broadcasted_iota(jnp.int32, choice.shape, 0)
    came = jnp.zeros(choice.shape, jnp.int32)
    for step in range(groups):
        reader = target(high, step, groups)
        slot = lax.rem(high - reader + groups, groups)
        owner = lax.rem(wanted_ref[0, reader * stride + low, slot], groups)
        came = jnp.where(row // groups == step, round_of(own, owner, groups), came)
    choice[...] = jnp.where(row % groups == came, 1.0, 0.0)
    row = lax.broadcasted_iota(jnp.int32, goals.shape, 0)
    goal = jnp.zeros(goals.shape, jnp.int32)
    for s in range(goals_ref.shape[2]):
        goal = jnp.where(row == s, goals_ref[0, 0, s], goal)
    goals[...] = goal.astype(jnp.float32)
    for load in loads:
        load.wait()


def pinned(array):
    return pltpu.with_memory_space_constraint(array, pltpu.HBM)


def pack(x_tiles, x2_tiles, x_cols, x2_cols, requests, out_cols, stride, spans):
    _, groups, stored, side, _ = x_tiles.shape
    kind = x_tiles.dtype
    small = (jnp.swapaxes(x_cols, 1, 2), jnp.swapaxes(x2_cols, 1, 2), requests, out_cols)
    shapes = [jax.ShapeDtypeStruct((rows_of(span, stored, side), side), kind) for cut in spans for span in cut]
    shapes += [
        jax.ShapeDtypeStruct((groups * groups, side), jnp.float32),
        jax.ShapeDtypeStruct((-(-out_cols.shape[2] // 8) * 8, side), jnp.float32),
    ]
    out = pl.pallas_call(
        functools.partial(pack_kernel, stride, spans),
        out_shape=shapes,
        in_specs=[HBM] * 6,
        out_specs=[VMEM] * len(shapes),
        scratch_shapes=[pltpu.SMEM(array.shape, array.dtype) for array in small]
        + [pltpu.SemaphoreType.DMA((groups, 2 * stored)), pltpu.SemaphoreType.DMA((len(small),))],
        compiler_params=SMALL,
        name="pack",
    )(pinned(x_tiles), pinned(x2_tiles), *map(pinned, small))
    flat = iter(out)
    return [[next(flat) for _ in cut] for cut in spans], *flat


def split_kernel(slots, slab_far, _, own_ref, *rest):
    outs, (wide, slab_ref, sems) = rest[:-3], rest[-3:]
    layers, pieces = len(outs) + 1, sems.shape[0]
    rows = slab_far.shape[0] // layers
    share = rows // pieces
    own, parity = lax.axis_index("layer"), lax.axis_index("col") % 2
    firsts = [target(own, step, layers) * rows for step in range(layers)]
    loads = [
        [
            pltpu.make_async_copy(
                slab_far.at[pl.ds(pl.multiple_of(first + at * share, share), share)],
                slab_ref.at[step, pl.ds(at * share, share)],
                sems.at[at, step],
            )
            for at in range(pieces)
        ]
        for step, first in enumerate(firsts)
    ]
    for load in sum(loads, []):
        load.start()
    for step in reversed(range(layers)):
        for load in loads[step]:
            load.wait()
        wide[...] = slab_ref[step].astype(jnp.float32)
        if step:
            half = slots // 2
            for slot in range(half):
                picked = wide[pl.ds(parity * half + slot, rows // slots, stride=slots)]
                outs[step - 1][slot] = picked.astype(own_ref.dtype)
        else:
            for slot in range(slots):
                own_ref[slot] = wide[pl.ds(slot, rows // slots, stride=slots)].astype(own_ref.dtype)


def split(slab_tiles, after, layers):
    high, per, _, slots, side = slab_tiles.shape
    rows = high * per // layers
    kind = slab_tiles.dtype
    out = pl.pallas_call(
        functools.partial(split_kernel, slots),
        out_shape=[jax.ShapeDtypeStruct((slots, rows, side), kind)]
        + [jax.ShapeDtypeStruct((slots // 2, rows, side), kind)] * (layers - 1),
        in_specs=[HBM, pl.BlockSpec(memory_space=pl.ANY)],
        out_specs=[VMEM] * layers,
        scratch_shapes=[
            pltpu.VMEM((rows * slots, side), jnp.float32),
            pltpu.VMEM((layers, rows * slots, side), kind),
            pltpu.SemaphoreType.DMA((4, layers)),
        ],
        compiler_params=SMALL,
        name="split",
    )(pinned(slab_tiles.reshape(high * per * slots, side)), after)
    return out[0], list(out[1:])


def pick_kernel(spans, wanted, stored, choice, *rest):
    held, outs = list(rest[: -len(wanted)]), rest[-len(wanted) :]
    held = [[held.pop(0) for _ in cut] for cut in spans]
    groups, side = len(held), choice.shape[1]
    count = id_rows(stored)
    for out, (step, span) in zip(outs, wanted):
        hits = [
            jnp.broadcast_to(choice[step * groups + at : step * groups + at + 1, :], (side, side)).astype(out.dtype)
            for at in range(groups)
        ]
        for block in range(*span):
            total = jnp.zeros((side, side), out.dtype)
            for at in range(groups):
                piece, first = find(held[at], spans[at], block, side)
                total += piece[pl.ds(first, side), :] * hits[at]
            out[pl.ds((block - span[0]) * side, side), :] = total
        if span[1] == 2 * stored:
            total = jnp.zeros((count, side), out.dtype)
            for at in range(groups):
                total += held[at][-1][pl.ds(held[at][-1].shape[0] - count, count), :] * hits[at][:count]
            out[pl.ds(out.shape[0] - count, count), :] = total


def pick(choice, held, spans, wanted, stored):
    side, kind = held[0][0].shape[1], held[0][0].dtype
    flat = [piece for block in held for piece in block]
    return pl.pallas_call(
        functools.partial(pick_kernel, spans, wanted, stored),
        out_shape=[jax.ShapeDtypeStruct((rows_of(span, stored, side), side), kind) for _, span in wanted],
        in_specs=[VMEM] * (1 + len(flat)),
        out_specs=[VMEM] * len(wanted),
        compiler_params=SMALL,
        name="pick",
    )(choice, *flat)


def product_kernel(stride, groups, layers, stored, items, wanted, last, goals, *rest):
    lefts, rest = rest[: 2 * layers - 1], list(rest[2 * layers - 1 :])
    slots, rows, side = lefts[0].shape
    half = slots // 2
    high, parity = lax.axis_index("row") // stride, lax.axis_index("col") % 2
    left_parts, sums = ([], []), ([], [])
    for layer in range(layers):
        for step, spans in items:
            slot = lax.rem(mate(high, step, groups) - high + groups, groups)
            if layer:
                same, other = lefts[2 * layer - 1], lefts[2 * layer]
                at = lax.rem(slot, half)
                left = jnp.where(slot // half == parity, same[at], other[at])
            else:
                left = lefts[0][slot]
            ids = rest.pop(0)
            digits = ids[pl.ds(ids.shape[0] - id_rows(stored), id_rows(stored)), :].astype(jnp.float32)
            pieces = [ids if span[1] == 2 * stored else rest.pop(0) for span in spans]
            for part in range(2):
                blocks = [b for low, high_ in spans for b in range(low, high_) if b // stored == part]
                if not blocks:
                    continue
                across = [jnp.zeros((side, side), jnp.bfloat16)] * wanted
                for block in blocks:
                    piece, first = find(pieces, spans, block, side)
                    tile = piece[pl.ds(first, side), :]
                    listed = (
                        digits[2 * block : 2 * block + 1] * (1 << DIGIT)
                        + digits[2 * block + 1 : 2 * block + 2]
                    )
                    for s in range(wanted):
                        hit = jnp.where(listed == goals[s : s + 1, :], 1.0, 0.0)
                        hit = jnp.broadcast_to(hit, (side, side))
                        across[s] = across[s] + tile * hit.astype(jnp.bfloat16)
                sums[part].append(jnp.concatenate(across, axis=1))
                left_parts[part].append(left)
    summed = None
    for factor, left, chosen in zip((4.0, -3.0), left_parts, sums):
        if left:
            term = factor * jnp.dot(
                jnp.concatenate(left, axis=1),
                jnp.concatenate(chosen, axis=0),
                preferred_element_type=jnp.float32,
            )
            summed = term if summed is None else summed + term
    if last:
        tall = rest.pop()
    out_ref = rest.pop()
    if rest:
        summed += rest.pop()[...]
    if last:
        for s in range(wanted):
            tall[pl.ds(s, rows, stride=wanted)] = summed[:, s * side : (s + 1) * side]
        summed = tall[...]
    out_ref[...] = summed.astype(out_ref.dtype)


def product(lefts, blocks, total, goals, wanted, stored, stride, items, last):
    layers, groups = len(blocks), len(blocks[0])
    _, rows, side = lefts[0].shape
    flat = []
    for of_layer in blocks:
        for step, spans in items:
            flat.append(of_layer[step][max(of_layer[step])])
            flat += [of_layer[step][span] for span in spans if span[1] < 2 * stored]
    flat += [] if total is None else [total]
    shape = (rows * wanted, side) if last else (rows, wanted * side)
    return pl.pallas_call(
        functools.partial(product_kernel, stride, groups, layers, stored, items, wanted, last),
        out_shape=jax.ShapeDtypeStruct(shape, lefts[0].dtype if last else jnp.float32),
        in_specs=[VMEM] * (1 + len(lefts) + len(flat)),
        out_specs=VMEM,
        scratch_shapes=[pltpu.VMEM(shape, jnp.float32)] if last else [],
        compiler_params=pltpu.CompilerParams(vmem_limit_bytes=16 * 1024 * 1024),
        name="product",
    )(goals, *lefts, *flat)


def body(slab_tiles, x_tiles, x_cols, x2_tiles, x2_cols, requests, out_cols):
    layers, rows, groups = (lax.axis_size(axis) for axis in ("layer", "row", "col"))
    stride = rows // groups
    _, _, stored, side, _ = x_tiles.shape
    all_blocks = (0, 2 * stored)
    col_cut, G = [all_blocks], {'seq': [('A',), ('pick', 0), ('z', 'far', 0), ('z', 'near', 0), ('z', 'last', 0), ('x', 'own', 0), ('x', 'far', 0), ('x', 'last', 0), ('x', 'near', 0)], 'split': ('y', 'near', 0), 'stages': [['far'], ['own', 'near'], ['last']], ('pick', 0): (('A',),), ('x', 'far', 0): (('x', 'own', 0),), ('x', 'near', 0): (('x', 'own', 0),), ('x', 'last', 0): (('x', 'own', 0),)}
    far = list(reversed(range(WHOLE, groups)))
    spans = [[all_blocks] if k < WHOLE else col_cut for k in range(groups)]
    row_cut = [[all_blocks] if k in far[:-1] else [all_blocks] if k >= WHOLE else [[all_blocks], [all_blocks]][k == 0] for k in range(groups)]
    done = {}

    def gated(value, names):
        after = [done[name] for name in names if name in done]
        return lax.optimization_barrier((value, after))[0] if after else value

    def label(k):
        return "own" if k == 0 else "near" if k < WHOLE else "far" if k != far[-1] else "last"

    packed, choice, goals = pack(x_tiles, x2_tiles, x_cols, x2_cols, requests, out_cols, stride, spans)
    held = [packed[0]] + [[exchange(piece, "col", k, groups) for piece in packed[k]] for k in range(1, groups)]
    for k in range(1, groups):
        for part, piece in enumerate(held[k]):
            done["y", label(k), part] = piece
    got = [{} for _ in range(groups)]
    blocks = [got] + [[{} for _ in range(groups)] for _ in range(1, layers)]

    def row(k, span, piece):
        name = ("z", label(k), row_cut[k].index(span))
        got[k][span] = done[name] = exchange(gated(piece, G.get(name, ())), "row", k, groups, stride)

    def forward(k, span):
        name = ("x", label(k), row_cut[k].index(span))
        piece = gated(got[k][span], G.get(name, ()))
        for step in range(1, layers):
            blocks[step][k][span] = done[name] = exchange(piece, "layer", step, layers)

    def slab():
        own, sent = split(slab_tiles, done[G["split"]], layers)
        sent = [exchange(gated(sent[k - 1], G.get(("A",), ())), "layer", k, layers) for k in range(1, layers)]
        done["A",] = sent[0]
        return [own] + [left for same in sent for left in (same, exchange(same, "col", 1, groups))]

    def choose(stage):
        low, high = col_cut[stage]
        wanted = [(k, span) for k in range(WHOLE) for span in row_cut[k] if stage == len(col_cut) - 1]
        wanted += [(k, span) for k in far for span in row_cut[k] if low < span[1] <= high]
        ready = [block if k < WHOLE else block[: stage + 1] for k, block in enumerate(held)]
        ready = gated(ready, G.get(("pick", stage), ()))
        here = [cut[: len(block)] for cut, block in zip(spans, ready)]
        picked = pick(choice, ready, here, wanted, stored)
        done["pick", stage] = picked[0]
        for (k, span), piece in zip(wanted, picked):
            chosen[k, span] = piece

    chosen, lefts = {}, None
    for token in G["seq"]:
        if token[0] == "pick":
            choose(token[1])
        elif token[0] == "A":
            lefts = slab()
        else:
            rounds = {"own": [0], "near": list(range(1, WHOLE)), "far": far[:-1], "last": far[-1:]}[token[1]]
            for k in rounds:
                span = row_cut[k][token[2]]
                if k == 0:
                    got[0][span] = chosen[0, span]
                if token[0] == "z":
                    row(k, span, chosen[k, span])
                else:
                    forward(k, span)

    def add(total, items, last):
        return product(lefts, blocks, total, goals, out_cols.shape[2], stored, stride, items, last)

    total = None
    for stage in G["stages"]:
        rounds = {"own": [0], "near": list(range(1, WHOLE)), "far": far[:-1], "last": far[-1:]}
        items = [(k, tuple(row_cut[k])) for name in stage for k in rounds[name]]
        total = add(total, items, stage is G["stages"][-1])
    high, per = slab_tiles.shape[0] // layers, slab_tiles.shape[1]
    return total.reshape(high, per, 1, out_cols.shape[2], side)


def solution(mesh):
    placed = (
        P(None, "row", "layer", None, None),
        P(("layer", "row", "col"), None, None, None, None),
        P(("layer", "row", "col"), None, None),
        P(("layer", "row", "col"), None, None, None, None),
        P(("layer", "row", "col"), None, None),
        P("layer", None, None),
        P("row", "col", None),
    )
    return jax.shard_map(
        body,
        mesh=mesh,
        in_specs=placed,
        out_specs=P("layer", "row", "col", None, None),
        check_vma=False,
    )
```

```python
import functools

import jax
import jax.numpy as jnp
from jax import lax
from jax.experimental import pallas as pl
from jax.experimental.pallas import tpu as pltpu
from jax.sharding import PartitionSpec as P

DIGIT = 8
SLACK = 8
VMEM = pl.BlockSpec(memory_space=pltpu.VMEM)
SMEM = pl.BlockSpec(memory_space=pltpu.SMEM)
HBM = pl.BlockSpec(memory_space=pltpu.HBM)
SMALL = pltpu.CompilerParams(vmem_limit_bytes=8 * 1024 * 1024)


def mate(index, step, size):
    return index ^ step if size & (size - 1) == 0 else (index - step) % size


def target(index, step, size):
    return index ^ step if size & (size - 1) == 0 else (index + step) % size


def round_of(index, source, size):
    return index ^ source if size & (size - 1) == 0 else lax.rem(index - source + size, size)


def exchange(block, axis, step, size, stride=1):
    route = []
    for place in range(size * stride):
        high, low = divmod(place, stride)
        route.append((place, target(high, step, size) * stride + low))
    return lax.ppermute(block, axis, route)


def gated(value, after):
    return lax.optimization_barrier((value, after))[0]


def id_rows(stored):
    return -(-4 * stored // 16) * 16


def pack_kernel(stride, x_far, x2_far, *rest):
    groups, stored, side = x_far.shape[1:4]
    fars, outs, (choice, goals) = rest[:4], rest[4 : 4 + groups], rest[4 + groups : 6 + groups]
    nears, (sems, id_sems) = rest[6 + groups : 10 + groups], rest[10 + groups :]
    cols_ref, cols2_ref, wanted_ref, goals_ref = nears
    count = id_rows(stored)
    own = lax.axis_index("col")
    ids = [
        pltpu.make_async_copy(far, near, id_sems.at[at]) for at, (far, near) in enumerate(zip(fars, nears))
    ]
    loads = [
        pltpu.make_async_copy(
            (x_far, x2_far)[block // stored].at[0, target(own, step, groups), block % stored],
            out.at[pl.ds(block * side, side)],
            sems.at[step, block],
        )
        for step, out in enumerate(outs)
        for block in range(2 * stored)
    ]
    for load in ids + loads:
        load.start()
    for load in ids:
        load.wait()
    row = lax.broadcasted_iota(jnp.int32, (count, side), 0)
    for step, out in enumerate(outs):
        reader = target(own, step, groups)
        digits = jnp.zeros((count, side), jnp.int32)
        for block in range(2 * stored):
            value = (cols_ref, cols2_ref)[block // stored][0, block % stored, reader]
            digits = jnp.where(row == 2 * block, value >> DIGIT, digits)
            digits = jnp.where(row == 2 * block + 1, value & ((1 << DIGIT) - 1), digits)
        out[pl.ds(2 * stored * side, count), :] = digits.astype(jnp.float32).astype(out.dtype)
    own_row = lax.axis_index("row")
    high, low = own_row // stride, own_row % stride
    row = lax.broadcasted_iota(jnp.int32, choice.shape, 0)
    came = jnp.zeros(choice.shape, jnp.int32)
    for step in range(groups):
        reader = target(high, step, groups)
        slot = lax.rem(high - reader + groups, groups)
        owner = lax.rem(wanted_ref[0, reader * stride + low, slot], groups)
        came = jnp.where(row // groups == step, round_of(own, owner, groups), came)
    choice[...] = jnp.where(row % groups == came, 1.0, 0.0)
    row = lax.broadcasted_iota(jnp.int32, goals.shape, 0)
    goal = jnp.zeros(goals.shape, jnp.int32)
    for s in range(goals_ref.shape[2]):
        goal = jnp.where(row == s, goals_ref[0, 0, s], goal)
    goals[...] = goal.astype(jnp.float32)
    for load in loads:
        load.wait()


def pinned(array):
    return pltpu.with_memory_space_constraint(array, pltpu.HBM)


def pack(x_tiles, x2_tiles, x_cols, x2_cols, requests, out_cols, stride):
    _, groups, stored, side, _ = x_tiles.shape
    small = (jnp.swapaxes(x_cols, 1, 2), jnp.swapaxes(x2_cols, 1, 2), requests, out_cols)
    shapes = [jax.ShapeDtypeStruct((2 * stored * side + id_rows(stored), side), x_tiles.dtype)] * groups
    shapes += [
        jax.ShapeDtypeStruct((groups * groups, side), jnp.float32),
        jax.ShapeDtypeStruct((-(-out_cols.shape[2] // 8) * 8, side), jnp.float32),
    ]
    out = pl.pallas_call(
        functools.partial(pack_kernel, stride),
        out_shape=shapes,
        in_specs=[HBM] * 6,
        out_specs=[VMEM] * len(shapes),
        scratch_shapes=[pltpu.SMEM(array.shape, array.dtype) for array in small]
        + [pltpu.SemaphoreType.DMA((groups, 2 * stored)), pltpu.SemaphoreType.DMA((len(small),))],
        compiler_params=SMALL,
        name="pack",
    )(pinned(x_tiles), pinned(x2_tiles), *map(pinned, small))
    return out[:groups], out[groups], out[groups + 1]


def split_kernel(slots, slab_far, _, own_ref, *rest):
    outs, (wide, slab_ref, sems) = rest[:-3], rest[-3:]
    layers, pieces = len(outs) + 1, sems.shape[0]
    rows = slab_far.shape[0] // layers
    share = rows // pieces
    own, parity = lax.axis_index("layer"), lax.axis_index("col") % 2
    firsts = [target(own, step, layers) * rows for step in range(layers)]
    loads = [
        [
            pltpu.make_async_copy(
                slab_far.at[pl.ds(pl.multiple_of(first + at * share, share), share)],
                slab_ref.at[step, pl.ds(at * share, share)],
                sems.at[at, step],
            )
            for at in range(pieces)
        ]
        for step, first in enumerate(firsts)
    ]
    for load in sum(loads, []):
        load.start()
    for step in reversed(range(layers)):
        for load in loads[step]:
            load.wait()
        wide[pl.ds(0, rows), :] = slab_ref[step].astype(jnp.float32)
        if step:
            half = slots // 2
            for slot in range(half):
                picked = wide[pl.ds(parity * half + slot, rows // slots, stride=slots)]
                outs[step - 1][slot] = picked.astype(own_ref.dtype)
        else:
            for slot in range(slots):
                own_ref[slot] = wide[pl.ds(slot, rows // slots, stride=slots)].astype(own_ref.dtype)


def split(slab_tiles, after, layers):
    high, per, _, slots, side = slab_tiles.shape
    rows = high * per // layers
    kind = slab_tiles.dtype
    out = pl.pallas_call(
        functools.partial(split_kernel, slots),
        out_shape=[jax.ShapeDtypeStruct((slots, rows, side), kind)]
        + [jax.ShapeDtypeStruct((slots // 2, rows, side), kind)] * (layers - 1),
        in_specs=[HBM, pl.BlockSpec(memory_space=pl.ANY)],
        out_specs=[VMEM] * layers,
        scratch_shapes=[
            pltpu.VMEM((rows * slots + SLACK, side), jnp.float32),
            pltpu.VMEM((layers, rows * slots, side), kind),
            pltpu.SemaphoreType.DMA((4, layers)),
        ],
        compiler_params=SMALL,
        name="split",
    )(pinned(slab_tiles.reshape(high * per * slots, side)), after)
    return out[0], list(out[1:])


def pick_kernel(rounds, choice, *rest):
    held, outs = rest[: -len(rounds)], rest[-len(rounds) :]
    groups = len(held)
    for out, step in zip(outs, rounds):
        total = jnp.zeros(out.shape, out.dtype)
        for at in range(groups):
            place = step * groups + at
            hit = jnp.broadcast_to(choice[place : place + 1, :], out.shape).astype(out.dtype)
            total += held[at][...] * hit
        out[...] = total


def pick(choice, held, rounds):
    shape = jax.ShapeDtypeStruct(held[0].shape, held[0].dtype)
    return pl.pallas_call(
        functools.partial(pick_kernel, rounds),
        out_shape=[shape] * len(rounds),
        in_specs=[VMEM] * (1 + len(held)),
        out_specs=[VMEM] * len(rounds),
        compiler_params=SMALL,
        name="pick",
    )(choice, *held)


def product_kernel(stride, groups, items, wanted, stored, layers, last, goals, *rest):
    lefts, rest = rest[: 2 * layers - 1], list(rest[2 * layers - 1 :])
    blocks, rest = rest[: len(items)], rest[len(items) :]
    slots, rows, side = lefts[0].shape
    half = slots // 2
    high, parity = lax.axis_index("row") // stride, lax.axis_index("col") % 2
    left_parts, sums = [], ([], [])
    for (layer, step), ref in zip(items, blocks):
        slot = lax.rem(mate(high, step, groups) - high + groups, groups)
        if layer:
            same, other = lefts[2 * layer - 1], lefts[2 * layer]
            at = lax.rem(slot, half)
            left_parts.append(jnp.where(slot // half == parity, same[at], other[at]))
        else:
            left_parts.append(lefts[0][slot])
        digits = ref[pl.ds(2 * stored * side, id_rows(stored)), :].astype(jnp.float32)
        for part, chosen in enumerate(sums):
            across = [jnp.zeros((side, side), ref.dtype)] * wanted
            for block in range(part * stored, (part + 1) * stored):
                tile = ref[pl.ds(block * side, side), :]
                listed = (
                    digits[2 * block : 2 * block + 1] * (1 << DIGIT) + digits[2 * block + 1 : 2 * block + 2]
                )
                for s in range(wanted):
                    hit = jnp.where(listed == goals[s : s + 1, :], 1.0, 0.0)
                    hit = jnp.broadcast_to(hit, (side, side))
                    across[s] = across[s] + tile * hit.astype(ref.dtype)
            chosen.append(jnp.concatenate(across, axis=1))
    left = jnp.concatenate(left_parts, axis=1)
    first, second = (jnp.concatenate(chosen, axis=0) for chosen in sums)

    def term(low, high):
        return 4.0 * jnp.dot(left[low:high], first, preferred_element_type=jnp.float32) - 3.0 * jnp.dot(
            left[low:high], second, preferred_element_type=jnp.float32
        )

    if not last:
        total = term(0, rows)
        rest[-1][...] = total + rest[0][...] if len(rest) > 1 else total
        return
    total, out_far, tall, out, sems = rest
    share = rows // sems.shape[0]
    copies = []
    for at in range(sems.shape[0]):
        summed = term(at * share, (at + 1) * share) + total[pl.ds(at * share, share), :]
        part = pl.ds(at * share * wanted, share * wanted)
        for s in range(wanted):
            tall[pl.ds(at * share * wanted + s, share, stride=wanted)] = summed[:, s * side : (s + 1) * side]
        out[part] = tall[part].astype(out.dtype)
        copies.append(pltpu.make_async_copy(out.at[part], out_far.at[part], sems.at[at]))
        copies[-1].start()
    for copy in copies:
        copy.wait()


def product(lefts, blocks, total, goals, wanted, stored, stride, items, last):
    layers, groups = len(blocks), len(blocks[0])
    _, rows, side = lefts[0].shape
    flat = [blocks[layer][step] for layer, step in items] + ([] if total is None else [total])
    shape, kind = ((rows * wanted, side), lefts[0].dtype) if last else ((rows, wanted * side), jnp.float32)
    scratch = [pltpu.VMEM((shape[0] + SLACK, side), jnp.float32), pltpu.VMEM(shape, kind), pltpu.SemaphoreType.DMA((2,))]
    return pl.pallas_call(
        functools.partial(product_kernel, stride, groups, items, wanted, stored, layers, last),
        out_shape=jax.ShapeDtypeStruct(shape, kind),
        in_specs=[VMEM] * (1 + len(lefts) + len(flat)),
        out_specs=HBM if last else VMEM,
        scratch_shapes=scratch if last else [],
        compiler_params=pltpu.CompilerParams(vmem_limit_bytes=16 * 1024 * 1024),
        name="product",
    )(goals, *lefts, *flat)


def body(slab_tiles, x_tiles, x_cols, x2_tiles, x2_cols, requests, out_cols):
    layers, rows, groups = (lax.axis_size(axis) for axis in ("layer", "row", "col"))
    stride = rows // groups
    _, _, stored, side, _ = x_tiles.shape
    wanted = out_cols.shape[2]
    packed, choice, goals = pack(x_tiles, x2_tiles, x_cols, x2_cols, requests, out_cols, stride)
    held = [packed[0]] + [exchange(packed[k], "col", k, groups) for k in range(1, groups)]
    own, sent = split(slab_tiles, held[1], layers)
    sent = [exchange(sent[k - 1], "layer", k, layers) for k in range(1, layers)]
    held, sent = lax.optimization_barrier((held, sent))
    lefts = [own] + [left for same in sent for left in (same, exchange(same, "col", 1, groups))]
    picked = pick(choice, held, list(range(groups)))
    order = [*reversed(range(2, groups)), 1]
    last = order[-2]
    got = [picked[0]] + [None] * (groups - 1)
    for k in order:
        got[k] = exchange(picked[k], "row", k, groups, stride)
    blocks = [got] + [[exchange(got[0], "layer", step, layers)] + [None] * (groups - 1) for step in range(1, layers)]
    for k in order:
        block = gated(got[k], blocks[-1][0])
        for step in range(1, layers):
            blocks[step][k] = exchange(block, "layer", step, layers)

    def add(total, rounds, parts, end=False):
        items = [(layer, k) for layer in parts for k in rounds]
        return product(lefts, blocks, total, goals, wanted, stored, stride, items, end)

    everywhere = range(layers)
    total = add(None, [k for k in order if k not in (1, last)], everywhere)
    total = add(total, [0, 1], everywhere)
    total = add(total, [last], everywhere[:1])
    total = add(total, [last], everywhere[1:], True)
    high, per = slab_tiles.shape[0] // layers, slab_tiles.shape[1]
    return total.reshape(high, per, 1, wanted, side)


def solution(mesh):
    placed = (
        P(None, "row", "layer", None, None),
        P(("layer", "row", "col"), None, None, None, None),
        P(("layer", "row", "col"), None, None),
        P(("layer", "row", "col"), None, None, None, None),
        P(("layer", "row", "col"), None, None),
        P("layer", None, None),
        P("row", "col", None),
    )
    return jax.shard_map(
        body,
        mesh=mesh,
        in_specs=placed,
        out_specs=P("layer", "row", "col", None, None),
        check_vma=False,
    )
```
